256 devices in a mesh: ctx: 16 (over z_hi, y, core), head: 16 (over z_lo, x).
Axes of the slice: x: 4, y: 4, z: 8 (z_hi: 2, z_lo: 4; z = z_hi * 4 + z_lo), core: 2. Of those that a mesh axis runs over, the one named last changes fastest.
Arguments:
- query: bfloat16 [7168, 4096], P('ctx', 'head'), may hold values from -80 to 80
- key_states: bfloat16 [7168, 1024], P('ctx'), may hold values from -4 to 4
- value_states: bfloat16 [7168, 1024], P('ctx'), may hold values from -6 to 6
- d_out: bfloat16 [7168, 4096], P('ctx', 'head'), may hold values from -6 to 6
- span_order: int32 [32], P('ctx'), may hold values from 0 to 31, each once
Outputs:
- d_query: bfloat16 [7168, 4096], P('ctx', 'head')
- d_key: bfloat16 [7168, 1024], P('ctx', 'head')
- d_value: bfloat16 [7168, 1024], P('ctx', 'head')
The draws below stay inside these ranges and needn't reach their ends.
All inputs are finite; a program needn't handle non-finite values.
Results may differ from the reference program's by a relative error of at most 0.007.
Values may be sent and summed in bfloat16 or wider, within the bound.
No kernel may reach another device: no remote copies, remote signals or barrier semaphores. Data moves between devices by JAX's collectives and lax.ppermute only.
A program may use at most 64 MiB of HBM per device.

```python
import jax
import jax.numpy as jnp
from jax import lax

HD = 128
CH = 224
TOKENS = 7168
SPANS = 32
HEADS = 32
KV_HEADS = 8


def shared_keys(key):
    return jnp.clip(jax.random.normal(key, (TOKENS, KV_HEADS * HD), jnp.float32), -4.0, 4.0)


def draw_key_states(key, part):
    base = shared_keys(key)
    return base.astype(jnp.bfloat16)


def draw_query(key, part):
    key = jax.random.fold_in(key, 12)
    values = jnp.clip(jax.random.normal(key, (TOKENS, HEADS * HD), jnp.float32), -4.0, 4.0)
    return values.astype(jnp.bfloat16)


def shard_levels(key, extent, shards, smallest, top_value):
    level = 1.0
    for axis_at, parts in shards:
        heights = jax.random.uniform(jax.random.fold_in(jax.random.fold_in(key, 6), axis_at), (parts,), jnp.float32, smallest / len(shards), top_value / len(shards))
        level = level * jnp.repeat(jnp.exp(heights), extent[axis_at] // parts).reshape((-1,) + (1,) * (len(extent) - 1 - axis_at))
    return level


def gaussian(own_key, dims, deviation, limit, split=(), kind=jnp.bfloat16):
    values = deviation * jax.random.normal(own_key, dims, jnp.float32)
    if split:
        values = values * shard_levels(own_key, dims, split, -0.22, 0.18)
    return jnp.clip(values, -limit, limit).astype(kind)


def setup_inputs(seed: int = 0) -> dict:
    keys = jax.random.split(jax.random.key(seed), 6)
    return {
        "query": draw_query(jax.random.fold_in(keys[5], 71), 0),
        "key_states": draw_key_states(jax.random.fold_in(keys[5], 71), 0),
        "value_states": gaussian(keys[2], (TOKENS, KV_HEADS * HD), 1.0, 6.0, ((0, 16),)),
        "d_out": gaussian(keys[3], (TOKENS, HEADS * HD), 1.0, 6.0, ((0, 16), (1, 16))),
        "span_order": jax.random.permutation(keys[4], SPANS).astype(jnp.int32),
    }


def reference(query, key_states, value_states, d_out, span_order):
    group = HEADS // KV_HEADS
    scale = HD ** -0.5
    rows = jnp.arange(TOKENS, dtype=jnp.int32)
    position = (span_order[rows // CH] * CH + rows % CH).astype(jnp.int32)
    visible = position[:, None] >= position[None, :]
    q_all = query.reshape(TOKENS, HEADS, HD).transpose(1, 0, 2)
    o_all = d_out.reshape(TOKENS, HEADS, HD).transpose(1, 0, 2)
    k_all = key_states.reshape(TOKENS, KV_HEADS, HD).transpose(1, 0, 2)
    v_all = value_states.reshape(TOKENS, KV_HEADS, HD).transpose(1, 0, 2)

    def one_head(index):
        q_head = q_all[index]
        o_head = o_all[index]
        k_head = k_all[index // group]
        v_head = v_all[index // group]
        score = jnp.dot(q_head, k_head.T, preferred_element_type=jnp.float32) * scale
        biggest = jnp.max(jnp.where(visible, score, -1e30), axis=1)
        total = jnp.sum(jnp.where(visible, jnp.exp(score - biggest[:, None]), 0.0), axis=1)
        lse = biggest + jnp.log(total)
        prob = jnp.where(visible, jnp.exp(score - lse[:, None]), 0.0)
        d_prob = jnp.dot(o_head, v_head.T, preferred_element_type=jnp.float32)
        delta = jnp.sum(prob * d_prob, axis=1)
        d_score = (prob * (d_prob - delta[:, None])).astype(jnp.bfloat16)
        prob_low = prob.astype(jnp.bfloat16)
        grad_q = jnp.dot(d_score, k_head, preferred_element_type=jnp.float32) * scale
        grad_k = jnp.dot(d_score.T, q_head, preferred_element_type=jnp.float32) * scale
        grad_v = jnp.dot(prob_low.T, o_head, preferred_element_type=jnp.float32)
        return grad_q, grad_k, grad_v

    grad_q, grad_k, grad_v = lax.map(one_head, jnp.arange(HEADS, dtype=jnp.int32))
    d_query = grad_q.transpose(1, 0, 2).reshape(TOKENS, HEADS * HD).astype(jnp.bfloat16)
    grad_k = grad_k.reshape(KV_HEADS, group, TOKENS, HD).sum(axis=1)
    grad_v = grad_v.reshape(KV_HEADS, group, TOKENS, HD).sum(axis=1)
    d_key = grad_k.transpose(1, 0, 2).reshape(TOKENS, KV_HEADS * HD).astype(jnp.bfloat16)
    d_value = grad_v.transpose(1, 0, 2).reshape(TOKENS, KV_HEADS * HD).astype(jnp.bfloat16)
    return d_query, d_key, d_value
```

```python
import functools
import math

import jax
import jax.numpy as jnp
from jax import lax
from jax.experimental import pallas as pl
from jax.experimental.pallas import tpu as pltpu
from jax.sharding import PartitionSpec as P

HD = 128
CH = 224
ROWS = 2 * CH
PAIR = 2 * ROWS
LANES = 2 * ROWS
TAG = 16
SCALE = HD ** (-0.5)
LOG2_SCALE = SCALE * math.log2(math.e)
HIDDEN = -3e38
LOWEST = -1e30
F32 = jnp.float32
BF16 = jnp.bfloat16
VMEM = pl.BlockSpec(memory_space=pltpu.VMEM)


def turned(block, step):
    route = [(i, i & 9 | ((i >> 1) + step & 3) << 1) for i in range(16)]
    return lax.ppermute(block, "ctx", route)


def core_swapped(block):
    return lax.ppermute(block, "ctx", [(i, i ^ 1) for i in range(16)])


def far_swapped(block):
    return lax.ppermute(block, "ctx", [(i, i ^ 8) for i in range(16)])


def pair_swapped(block):
    return lax.ppermute(block, "head", [(i, i ^ 1) for i in range(16)])


def tagged(block, span_order):
    row = lax.broadcasted_iota(jnp.int32, (TAG, block.shape[1]), 0)
    tag = jnp.where(row == 0, span_order[0], jnp.where(row == 1, span_order[1], 0))
    return jnp.concatenate([block, tag.astype(BF16)], axis=0)


def dot(a, b, dims):
    return lax.dot_general(a, b, (dims, ((), ())), preferred_element_type=F32)


def tags(ref):
    rows = ref[ROWS : ROWS + TAG, :HD].astype(F32)
    wide = [jnp.concatenate([rows[i : i + 1]] * (LANES // HD), axis=1) for i in range(2)]
    return [w.astype(jnp.int32) * CH for w in wide]


def row_positions(ref):
    low, high = tags(ref)
    lane = lax.broadcasted_iota(jnp.int32, (1, LANES), 1)
    lane = jnp.where(lane >= ROWS, lane - ROWS, lane)
    return jnp.where(lane >= CH, high + lane - CH, low + lane)


def stacked(ref, at):
    return jnp.concatenate([ref[:ROWS, at : at + HD], ref[:ROWS, at + HD : at + 2 * HD]], axis=0)


def pair_of(near, far):
    k = jnp.concatenate([near[:ROWS, :HD], far[:ROWS, :HD]], axis=0)
    v = jnp.concatenate([near[:ROWS, HD:], far[:ROWS, HD:]], axis=0)
    starts = tags(near) + tags(far)
    return k, v, starts


def total_kernel(*refs):
    qo, stat = refs[0], refs[-1]
    blocks = refs[1:-1]
    q, o = stacked(qo, 0), stacked(qo, 2 * HD)
    at = row_positions(qo)
    key_row = lax.broadcasted_iota(jnp.int32, (CH, LANES), 0)
    biggest = jnp.full((8, LANES), LOWEST, F32)
    summed = jnp.zeros((8, LANES), F32)
    weighted = jnp.zeros((8, LANES), F32)
    for near, far in zip(blocks[0::2], blocks[1::2]):
        k, v, starts = pair_of(near, far)
        score = dot(k, q, ((1,), (1,)))
        d_prob = dot(v, o, ((1,), (1,)))
        parts = []
        newest = biggest
        for j, start in enumerate(starts):
            part = score[j * CH : (j + 1) * CH] * LOG2_SCALE
            part = jnp.where(key_row <= at - start, part, HIDDEN).reshape(CH // 8, 8, LANES)
            newest = jnp.maximum(newest, jnp.max(part, axis=0))
            parts.append(part)
        factor = jnp.exp2(biggest - newest)
        summed = summed * factor
        weighted = weighted * factor
        biggest = newest
        for j, part in enumerate(parts):
            expo = jnp.exp2(part - newest[None])
            summed += jnp.sum(expo, axis=0)
            weighted += jnp.sum(expo * d_prob[j * CH : (j + 1) * CH].reshape(CH // 8, 8, LANES), axis=0)
    top = jnp.max(biggest, axis=0, keepdims=True)
    factor = jnp.exp2(biggest - top)
    stat[0:1] = top
    stat[1:2] = jnp.sum(summed * factor, axis=0, keepdims=True)
    stat[2:3] = jnp.sum(weighted * factor, axis=0, keepdims=True)
    stat[3:8] = jnp.zeros((5, LANES), F32)


def totals(qo, blocks):
    pairs = len(blocks) // 2
    return pl.pallas_call(
        total_kernel,
        out_shape=jax.ShapeDtypeStruct((8, LANES), F32),
        in_specs=[VMEM] * (1 + len(blocks)),
        out_specs=VMEM,
        compiler_params=pltpu.CompilerParams(vmem_limit_bytes=48 << 20),
        cost_estimate=pl.CostEstimate(
            flops=pairs * 4 * PAIR * LANES * HD, bytes_accessed=pairs * 4 * PAIR * HD, transcendentals=pairs * PAIR * LANES
        ),
        name="totals",
    )(qo, *blocks)


def merged(here, there):
    top = jnp.maximum(here[0:1], there[0:1])
    mine, other = jnp.exp2(here[0:1] - top), jnp.exp2(there[0:1] - top)
    summed = here[1:2] * mine + there[1:2] * other
    weighted = here[2:3] * mine + there[2:3] * other
    return top + jnp.log2(summed), weighted / summed


def grad_kernel(first, last, *refs):
    qos, heres, theres, refs = refs[0:2], refs[2:4], refs[4:6], refs[6:]
    near, far, refs = refs[0], refs[1], refs[2:]
    if not first:
        old, refs = refs[0], refs[1:]
    own_part, far_part, dq_out = refs[0], refs[1], refs[2:]
    k, v, starts = pair_of(near, far)
    key_row = lax.broadcasted_iota(jnp.int32, (CH, LANES), 0)
    grad_k = grad_v = None
    for which in range(2):
        qo = qos[which]
        q, o = stacked(qo, 0), stacked(qo, 2 * HD)
        at = row_positions(qo)
        lse, delta = merged(heres[which], theres[which])
        score = dot(k, q, ((1,), (1,)))
        d_prob = dot(v, o, ((1,), (1,)))
        probs, d_scores = [], []
        for j, start in enumerate(starts):
            here = slice(j * CH, (j + 1) * CH)
            prob = jnp.exp2(score[here] * LOG2_SCALE - lse)
            prob = jnp.where(key_row <= at - start, prob, 0.0)
            d_scores.append((prob * (d_prob[here] - delta)).astype(BF16))
            probs.append(prob.astype(BF16))
        d_score = jnp.concatenate(d_scores, axis=0)
        prob = jnp.concatenate(probs, axis=0)
        term_k, term_v = dot(d_score, q, ((1,), (0,))), dot(prob, o, ((1,), (0,)))
        grad_k = term_k if grad_k is None else grad_k + term_k
        grad_v = term_v if grad_v is None else grad_v + term_v
        grad_q = dot(k, d_score, ((0,), (0,)))
        if not first:
            grad_q += old[which]
        if last:
            rows = (grad_q * SCALE).T
            dq_out[which][:, :HD] = rows[:ROWS].astype(dq_out[which].dtype)
            dq_out[which][:, HD:] = rows[ROWS:].astype(dq_out[which].dtype)
        else:
            dq_out[0][which] = grad_q
    own_part[:, :HD] = grad_k[:ROWS] * SCALE
    own_part[:, HD:] = grad_v[:ROWS]
    far_part[:, :HD] = (grad_k[ROWS:] * SCALE).astype(BF16)
    far_part[:, HD:] = grad_v[ROWS:].astype(BF16)


def grads(qos, heres, theres, near, far, old, last):
    first = old is None
    operands = [*qos, *heres, *theres, near, far] + ([] if first else [old])
    shape = jax.ShapeDtypeStruct
    dq_shapes = (
        [shape((ROWS, 2 * HD), F32), shape((ROWS, 2 * HD), BF16)] if last else [shape((2, HD, LANES), F32)]
    )
    return pl.pallas_call(
        functools.partial(grad_kernel, first, last),
        out_shape=[shape((ROWS, 2 * HD), F32), shape((ROWS, 2 * HD), BF16)] + dq_shapes,
        in_specs=[VMEM] * len(operands),
        out_specs=[VMEM] * (2 + len(dq_shapes)),
        compiler_params=pltpu.CompilerParams(vmem_limit_bytes=48 << 20),
        cost_estimate=pl.CostEstimate(
            flops=20 * PAIR * LANES * HD, bytes_accessed=16 * PAIR * HD, transcendentals=2 * PAIR * LANES
        ),
        name="grads",
    )(*operands)


def on_device(query, key_states, value_states, d_out, span_order):
    head_index = lax.axis_index("head")
    kv_index = head_index // 2
    k_own = lax.dynamic_slice_in_dim(key_states, kv_index * HD, HD, 1)
    v_own = lax.dynamic_slice_in_dim(value_states, kv_index * HD, HD, 1)
    kv = tagged(jnp.concatenate([k_own, v_own], axis=1), span_order)
    qo = tagged(jnp.concatenate([query, d_out], axis=1), span_order)
    qo_far = far_swapped(qo)
    back, ahead, across = turned(kv, 1), turned(kv, 3), turned(kv, 2)
    near = [kv, back, ahead, across]
    far = [core_swapped(block) for block in near]
    blocks = [b for pair in zip(near, far) for b in pair]
    here = totals(qo, blocks)
    here_at_far = far_swapped(here)
    there = totals(qo_far, blocks)
    there_at_far = far_swapped(there)
    qos, heres, theres = (qo, qo_far), (here, there), (there_at_far, here_at_far)

    arrived = []
    dq = None
    for at, step in ((3, 2), (1, 3), (2, 1)):
        own_part, far_part, dq = grads(qos, heres, theres, near[at], far[at], dq, False)
        part = own_part + core_swapped(far_part).astype(F32)
        arrived.append(turned(part.astype(BF16), step))
    own_part, far_part, dq_own, dq_far = grads(qos, heres, theres, near[0], far[0], dq, True)
    d_query = (dq_own + far_swapped(dq_far).astype(F32)).astype(BF16)
    mine = own_part + core_swapped(far_part).astype(F32)
    for part in arrived:
        mine = mine + part.astype(F32)
    half = HD // 2
    keep_at = head_index % 2 * half
    give_at = half - keep_at

    def cut(at):
        return [lax.dynamic_slice_in_dim(mine, first + at, half, 1) for first in (0, HD)]

    incoming = pair_swapped(jnp.concatenate(cut(give_at), axis=1).astype(BF16)).astype(F32)
    d_key, d_value = cut(keep_at)
    d_key = (d_key + incoming[:, :half]).astype(BF16)
    d_value = (d_value + incoming[:, half:]).astype(BF16)
    return d_query, d_key, d_value


def solution(mesh):
    return jax.shard_map(
        on_device,
        mesh=mesh,
        in_specs=(P("ctx", "head"), P("ctx", None), P("ctx", None), P("ctx", "head"), P("ctx")),
        out_specs=(P("ctx", "head"), P("ctx", "head"), P("ctx", "head")),
        check_vma=False,
    )
```

```python
import functools
import math

import jax
import jax.numpy as jnp
from jax import lax
from jax.experimental import pallas as pl
from jax.experimental.pallas import tpu as pltpu
from jax.sharding import PartitionSpec as P

HD = 128
CH = 224
ROWS = 2 * CH
PAIR = 2 * ROWS
LANES = 2 * ROWS
TAG = 16
LIMIT = 28
SCALE = HD ** (-0.5)
LOG2_SCALE = SCALE * math.log2(math.e)
HIDDEN = -3e38
LOWEST = -1e30
F32 = jnp.float32
BF16 = jnp.bfloat16
VMEM = pl.BlockSpec(memory_space=pltpu.VMEM)


def turned(block, step):
    route = [(i, i & 9 | ((i >> 1) + step & 3) << 1) for i in range(16)]
    return lax.ppermute(block, "ctx", route)


def core_swapped(block):
    return lax.ppermute(block, "ctx", [(i, i ^ 1) for i in range(16)])


def far_swapped(block):
    return lax.ppermute(block, "ctx", [(i, i ^ 8) for i in range(16)])


def pair_swapped(block):
    return lax.ppermute(block, "head", [(i, i ^ 1) for i in range(16)])


def tagged(span_order, *sides):
    width = sum(side.shape[1] for side in sides)
    tag = jnp.broadcast_to(jnp.pad(span_order.astype(BF16), (0, TAG - 2))[:, None], (TAG, width))
    return jnp.concatenate([jnp.concatenate(sides, axis=1), tag], axis=0)


def dot(a, b, dims):
    return lax.dot_general(a, b, (dims, ((), ())), preferred_element_type=F32)


def tags(ref):
    rows = ref[ROWS : ROWS + TAG, :HD].astype(F32)
    wide = [jnp.concatenate([rows[i : i + 1]] * (LANES // HD), axis=1) for i in range(2)]
    return [w.astype(jnp.int32) * CH for w in wide]


def row_positions(ref):
    low, high = tags(ref)
    lane = lax.broadcasted_iota(jnp.int32, (1, LANES), 1)
    lane = jnp.where(lane >= ROWS, lane - ROWS, lane)
    return jnp.where(lane >= CH, high + lane - CH, low + lane)


def stacked(ref, at):
    return jnp.concatenate([ref[:ROWS, at : at + HD], ref[:ROWS, at + HD : at + 2 * HD]], axis=0)


def pair_of(near, far):
    k = jnp.concatenate([near[:ROWS, :HD], far[:ROWS, :HD]], axis=0)
    v = jnp.concatenate([near[:ROWS, HD:], far[:ROWS, HD:]], axis=0)
    starts = tags(near) + tags(far)
    return k, v, starts


def total_kernel(gather, *refs):
    qo, refs = refs[0], refs[1:]
    if gather:
        blocks, stat, kv = refs[:8], refs[8], refs[9]
        for i, block in enumerate(blocks):
            kv[i] = block[...]
    else:
        kv, earlier, stat = refs
        stat[:8] = earlier[...]
        stat = stat.at[8:16]
    q, o = stacked(qo, 0), stacked(qo, 2 * HD)
    at = row_positions(qo)
    key_row = lax.broadcasted_iota(jnp.int32, (CH, LANES), 0)

    def step(i, state):
        biggest, summed, weighted = state
        k, v, starts = pair_of(kv.at[2 * i], kv.at[2 * i + 1])
        score = dot(k, q, ((1,), (1,)))
        d_prob = dot(v, o, ((1,), (1,)))
        parts = []
        newest = biggest
        for j, start in enumerate(starts):
            part = score[j * CH : (j + 1) * CH] * LOG2_SCALE
            part = jnp.where(key_row <= at - start, part, HIDDEN).reshape(CH // 8, 8, LANES)
            newest = jnp.maximum(newest, jnp.max(part, axis=0))
            parts.append(part)
        factor = jnp.exp2(biggest - newest)
        summed = summed * factor
        weighted = weighted * factor
        for j, part in enumerate(parts):
            expo = jnp.exp2(part - newest[None])
            summed += jnp.sum(expo, axis=0)
            weighted += jnp.sum(expo * d_prob[j * CH : (j + 1) * CH].reshape(CH // 8, 8, LANES), axis=0)
        return newest, summed, weighted

    nothing = jnp.zeros((8, LANES), F32)
    biggest, summed, weighted = lax.fori_loop(0, 4, step, (nothing + LOWEST, nothing, nothing))
    top = jnp.max(biggest, axis=0, keepdims=True)
    factor = jnp.exp2(biggest - top)
    stat[0:1] = top
    stat[1:2] = jnp.sum(summed * factor, axis=0, keepdims=True)
    stat[2:3] = jnp.sum(weighted * factor, axis=0, keepdims=True)
    stat[3:8] = jnp.zeros((5, LANES), F32)


def call(kernel, name, outs, *operands):
    return pl.pallas_call(
        kernel,
        out_shape=[jax.ShapeDtypeStruct(*out) for out in outs],
        in_specs=[VMEM] * len(operands),
        out_specs=[VMEM] * len(outs),
        compiler_params=pltpu.CompilerParams(vmem_limit_bytes=LIMIT << 20),
        cost_estimate=pl.CostEstimate(flops=1 << 20, bytes_accessed=1 << 16, transcendentals=0),
        name=name,
    )(*operands)


def merged(here, there):
    top = jnp.maximum(here[0:1], there[0:1])
    mine, other = jnp.exp2(here[0:1] - top), jnp.exp2(there[0:1] - top)
    summed = here[1:2] * mine + there[1:2] * other
    weighted = here[2:3] * mine + there[2:3] * other
    return top + jnp.log2(summed), weighted / summed


def rows_of(qo, here, there):
    return stacked(qo, 0), stacked(qo, 2 * HD), row_positions(qo), *merged(here, there)


def tile(rows, near, far):
    q, o, at, lse, delta = rows
    k, v, starts = pair_of(near, far)
    key_row = lax.broadcasted_iota(jnp.int32, (CH, LANES), 0)
    score = dot(k, q, ((1,), (1,)))
    d_prob = dot(v, o, ((1,), (1,)))
    probs, d_scores = [], []
    for j, start in enumerate(starts):
        here = slice(j * CH, (j + 1) * CH)
        prob = jnp.exp2(score[here] * LOG2_SCALE - lse)
        prob = jnp.where(key_row <= at - start, prob, 0.0)
        d_scores.append((prob * (d_prob[here] - delta)).astype(BF16))
        probs.append(prob.astype(BF16))
    d_score = jnp.concatenate(d_scores, axis=0)
    prob = jnp.concatenate(probs, axis=0)
    return (
        dot(d_score, q, ((1,), (0,))) * SCALE,
        dot(prob, o, ((1,), (0,))),
        dot(k, d_score, ((0,), (0,))) * SCALE,
    )


def split_pair(term_k, term_v, own_part, far_part):
    own_part[:, :HD] = term_k[:ROWS]
    own_part[:, HD:] = term_v[:ROWS]
    far_part[:, :HD] = term_k[ROWS:].astype(BF16)
    far_part[:, HD:] = term_v[ROWS:].astype(BF16)


def put_rows(out, dq):
    rows = dq.T
    out[:, :HD] = rows[:ROWS].astype(out.dtype)
    out[:, HD:] = rows[ROWS:].astype(out.dtype)


def pair_kernel(place, qo, qo_far, stats, stats_far, kv, *refs):
    own_part, far_part, dq, dq_far = refs[-4:]
    old, old_far = refs[:2] if len(refs) > 4 else (None, None)
    near, far = kv.at[2 * place], kv.at[2 * place + 1]
    far_k, far_v, far_q = tile(rows_of(qo_far, stats[8:16], stats_far[0:8]), near, far)
    dq_far[...] = far_q if old is None else old_far[...] + far_q
    term_k, term_v, term_q = tile(rows_of(qo, stats[0:8], stats_far[8:16]), near, far)
    dq[...] = term_q if old is None else old[...] + term_q
    split_pair(term_k + far_k, term_v + far_v, own_part, far_part)


def far_kernel(qo_far, stats, stats_far, kv, dq, out, terms):
    term_k, term_v, term_q = tile(rows_of(qo_far, stats[8:16], stats_far[0:8]), kv.at[0], kv.at[1])
    put_rows(out, dq[...] + term_q)
    terms[:, :HD] = term_k
    terms[:, HD:] = term_v


def last_kernel(qo, stats, stats_far, kv, dq, terms, own_part, far_part, out):
    term_k, term_v, term_q = tile(rows_of(qo, stats[0:8], stats_far[8:16]), kv.at[0], kv.at[1])
    put_rows(out, dq[...] + term_q)
    split_pair(term_k + terms[:, :HD], term_v + terms[:, HD:], own_part, far_part)


def finish_kernel(dq, dq_far, kept, incoming, d_query, d_key, d_value):
    d_query[...] = (dq[...] + dq_far[...].astype(F32)).astype(BF16)
    both = (kept[...] + incoming[...].astype(F32)).T
    d_key[...] = both[: HD // 2].astype(BF16)
    d_value[...] = both[HD // 2 :].astype(BF16)


def on_device(query, key_states, value_states, d_out, span_order):
    head_index = lax.axis_index("head")
    first = head_index // 2 * HD
    k_own = lax.dynamic_slice_in_dim(key_states, first, HD, 1)
    v_own = lax.dynamic_slice_in_dim(value_states, first, HD, 1)
    kv = tagged(span_order, k_own, v_own)
    qo = tagged(span_order, query, d_out)
    qo_far = far_swapped(qo)
    near = [kv, turned(kv, 1), turned(kv, 3), turned(kv, 2)]
    far = [core_swapped(block) for block in near]
    blocks = [b for pair in zip(near, far) for b in pair]
    gathered = ((8, ROWS + TAG, 2 * HD), BF16)
    here, kv = call(functools.partial(total_kernel, True), "totals", [((8, LANES), F32), gathered], qo, *blocks)
    qo_far, kv = lax.optimization_barrier((qo_far, kv))
    (stats,) = call(functools.partial(total_kernel, False), "totals", [((16, LANES), F32)], qo_far, kv, here)
    stats_far = far_swapped(stats)
    halves = [((ROWS, 2 * HD), F32), ((ROWS, 2 * HD), BF16)]
    transposed = [((HD, LANES), F32)] * 2

    def grads(place, *before):
        kernel = functools.partial(pair_kernel, place)
        return call(kernel, "grads", halves + transposed, qo, qo_far, stats, stats_far, kv, *before)

    def joined(own_part, far_part):
        return (own_part + core_swapped(far_part).astype(F32)).astype(BF16)

    *part_a, dq, dq_far = grads(3)
    *part_b, dq, dq_far = grads(2, dq, dq_far)
    *part_c, dq, dq_far = grads(1, dq, dq_far)
    part_a = joined(*part_a)
    dq_far, part_a = lax.optimization_barrier((dq_far, part_a))
    part_a = turned(part_a, 2)
    far_outs = [((ROWS, 2 * HD), BF16), ((PAIR, 2 * HD), F32)]
    dq_far, terms = call(far_kernel, "far", far_outs, qo_far, stats, stats_far, kv, dq_far)
    part_b = joined(*part_b)
    dq, part_b, terms = lax.optimization_barrier((dq, part_b, terms))
    part_b = turned(part_b, 1)
    own_part, far_part, dq = call(last_kernel, "last", halves + halves[:1], qo, stats, stats_far, kv, dq, terms)
    arrived = [part_a, part_b, turned(joined(*part_c), 3)]
    dq_far = far_swapped(dq_far)
    grad = own_part + core_swapped(far_part).astype(F32)
    for part in arrived:
        grad = grad + part.astype(F32)
    half = HD // 2
    keep_at = head_index % 2 * half
    give_at = half - keep_at

    def cut(at):
        return jnp.concatenate([lax.dynamic_slice_in_dim(grad, first + at, half, 1) for first in (0, HD)], axis=1)

    incoming = pair_swapped(cut(give_at).astype(BF16))
    outs = [((ROWS, 2 * HD), BF16)] + [((half, ROWS), BF16)] * 2
    d_query, d_key, d_value = call(finish_kernel, "finish", outs, dq, dq_far, cut(keep_at), incoming)
    return d_query, d_key.T, d_value.T


def solution(mesh):
    return jax.shard_map(
        on_device,
        mesh=mesh,
        in_specs=(P("ctx", "head"), P("ctx", None), P("ctx", None), P("ctx", "head"), P("ctx")),
        out_specs=(P("ctx", "head"), P("ctx", "head"), P("ctx", "head")),
        check_vma=False,
    )
```

```python
import functools
import math

import jax
import jax.numpy as jnp
from jax import lax
from jax.experimental import pallas as pl
from jax.experimental.pallas import tpu as pltpu
from jax.sharding import PartitionSpec as P

HD = 128
CH = 224
ROWS = 2 * CH
PAIR = 2 * ROWS
LANES = 2 * ROWS
TAG = 16
LIMIT = 28
SCALE = HD ** (-0.5)
LOG2_SCALE = SCALE * math.log2(math.e)
HIDDEN = -3e38
LOWEST = -1e30
F32 = jnp.float32
BF16 = jnp.bfloat16
VMEM = pl.BlockSpec(memory_space=pltpu.VMEM)


def turned(block, step):
    route = [(i, i & 9 | ((i >> 1) + step & 3) << 1) for i in range(16)]
    return lax.ppermute(block, "ctx", route)


def core_swapped(block):
    return lax.ppermute(block, "ctx", [(i, i ^ 1) for i in range(16)])


def far_swapped(block):
    return lax.ppermute(block, "ctx", [(i, i ^ 8) for i in range(16)])


def pair_swapped(block):
    return lax.ppermute(block, "head", [(i, i ^ 1) for i in range(16)])


def tagged(span_order, *sides):
    width = sum(side.shape[1] for side in sides)
    tag = jnp.broadcast_to(jnp.pad(span_order.astype(BF16), (0, TAG - 2))[:, None], (TAG, width))
    return jnp.concatenate([jnp.concatenate(sides, axis=1), tag], axis=0)


def dot(a, b, dims):
    return lax.dot_general(a, b, (dims, ((), ())), preferred_element_type=F32)


def tags(ref):
    rows = ref[ROWS : ROWS + TAG, :HD].astype(F32)
    wide = [jnp.concatenate([rows[i : i + 1]] * (LANES // HD), axis=1) for i in range(2)]
    return [w.astype(jnp.int32) * CH for w in wide]


def row_positions(ref):
    low, high = tags(ref)
    lane = lax.broadcasted_iota(jnp.int32, (1, LANES), 1)
    lane = jnp.where(lane >= ROWS, lane - ROWS, lane)
    return jnp.where(lane >= CH, high + lane - CH, low + lane)


def stacked(ref, at):
    return jnp.concatenate([ref[:ROWS, at : at + HD], ref[:ROWS, at + HD : at + 2 * HD]], axis=0)


def pair_of(near, far):
    k = jnp.concatenate([near[:ROWS, :HD], far[:ROWS, :HD]], axis=0)
    v = jnp.concatenate([near[:ROWS, HD:], far[:ROWS, HD:]], axis=0)
    starts = tags(near) + tags(far)
    return k, v, starts


def total_kernel(gather, *refs):
    qo, refs = refs[0], refs[1:]
    if gather:
        blocks, stat, kv = refs[:8], refs[8], refs[9]
        for i, block in enumerate(blocks):
            kv[i] = block[...]
    else:
        kv, stat = refs
    q, o = stacked(qo, 0), stacked(qo, 2 * HD)
    at = row_positions(qo)
    key_row = lax.broadcasted_iota(jnp.int32, (CH, LANES), 0)

    def step(i, state):
        biggest, summed, weighted = state
        k, v, starts = pair_of(kv.at[2 * i], kv.at[2 * i + 1])
        score = dot(k, q, ((1,), (1,)))
        d_prob = dot(v, o, ((1,), (1,)))
        parts = []
        newest = biggest
        for j, start in enumerate(starts):
            part = score[j * CH : (j + 1) * CH] * LOG2_SCALE
            part = jnp.where(key_row <= at - start, part, HIDDEN).reshape(CH // 8, 8, LANES)
            newest = jnp.maximum(newest, jnp.max(part, axis=0))
            parts.append(part)
        factor = jnp.exp2(biggest - newest)
        summed = summed * factor
        weighted = weighted * factor
        for j, part in enumerate(parts):
            expo = jnp.exp2(part - newest[None])
            summed += jnp.sum(expo, axis=0)
            weighted += jnp.sum(expo * d_prob[j * CH : (j + 1) * CH].reshape(CH // 8, 8, LANES), axis=0)
        return newest, summed, weighted

    nothing = jnp.zeros((8, LANES), F32)
    biggest, summed, weighted = lax.fori_loop(0, 4, step, (nothing + LOWEST, nothing, nothing))
    top = jnp.max(biggest, axis=0, keepdims=True)
    factor = jnp.exp2(biggest - top)
    stat[0:1] = top
    stat[1:2] = jnp.sum(summed * factor, axis=0, keepdims=True)
    stat[2:3] = jnp.sum(weighted * factor, axis=0, keepdims=True)
    stat[3:8] = jnp.zeros((5, LANES), F32)


def call(kernel, name, outs, *operands):
    return pl.pallas_call(
        kernel,
        out_shape=[jax.ShapeDtypeStruct(*out) for out in outs],
        in_specs=[VMEM] * len(operands),
        out_specs=[VMEM] * len(outs),
        compiler_params=pltpu.CompilerParams(vmem_limit_bytes=LIMIT << 20),
        cost_estimate=pl.CostEstimate(flops=1 << 20, bytes_accessed=1 << 16, transcendentals=0),
        name=name,
    )(*operands)


def merged(here, there):
    top = jnp.maximum(here[0:1], there[0:1])
    mine, other = jnp.exp2(here[0:1] - top), jnp.exp2(there[0:1] - top)
    summed = here[1:2] * mine + there[1:2] * other
    weighted = here[2:3] * mine + there[2:3] * other
    return top + jnp.log2(summed), weighted / summed


def rows_of(qo, here, there):
    return stacked(qo, 0), stacked(qo, 2 * HD), row_positions(qo), *merged(here, there)


def tile(rows, near, far):
    q, o, at, lse, delta = rows
    k, v, starts = pair_of(near, far)
    key_row = lax.broadcasted_iota(jnp.int32, (CH, LANES), 0)
    score = dot(k, q, ((1,), (1,)))
    d_prob = dot(v, o, ((1,), (1,)))
    probs, d_scores = [], []
    for j, start in enumerate(starts):
        here = slice(j * CH, (j + 1) * CH)
        prob = jnp.exp2(score[here] * LOG2_SCALE - lse)
        prob = jnp.where(key_row <= at - start, prob, 0.0)
        d_scores.append((prob * (d_prob[here] - delta)).astype(BF16))
        probs.append(prob.astype(BF16))
    d_score = jnp.concatenate(d_scores, axis=0)
    prob = jnp.concatenate(probs, axis=0)
    return (
        dot(d_score, q, ((1,), (0,))) * SCALE,
        dot(prob, o, ((1,), (0,))),
        dot(k, d_score, ((0,), (0,))) * SCALE,
    )


def split_pair(term_k, term_v, own_part, far_part):
    own_part[:, :HD] = term_k[:ROWS]
    own_part[:, HD:] = term_v[:ROWS]
    far_part[:, :HD] = term_k[ROWS:].astype(BF16)
    far_part[:, HD:] = term_v[ROWS:].astype(BF16)


def put_rows(out, dq):
    rows = dq.T
    out[:, :HD] = rows[:ROWS].astype(out.dtype)
    out[:, HD:] = rows[ROWS:].astype(out.dtype)


def far_kernel(places, qo_far, here, there, kv, *refs):
    old, refs = (refs[0], refs[1:]) if len(refs) > 3 else (None, refs)
    out, *terms = refs
    rows = rows_of(qo_far, here, there)
    total = None if old is None else old[...]
    for place, wide in zip(places, terms):
        term_k, term_v, term_q = tile(rows, kv.at[2 * place], kv.at[2 * place + 1])
        wide[:, :HD] = term_k
        wide[:, HD:] = term_v
        total = term_q if total is None else total + term_q
    if places[-1] == 0:
        put_rows(out, total)
    else:
        out[...] = total


def own_kernel(places, qo, here, there, kv, *refs):
    terms, refs = refs[: len(places)], refs[len(places) :]
    own_part, far_part, out = refs[-3:]
    rows = rows_of(qo, here, there)
    total = refs[0][...] if len(refs) > 3 else None
    for i, (place, wide) in enumerate(zip(places, terms)):
        term_k, term_v, term_q = tile(rows, kv.at[2 * place], kv.at[2 * place + 1])
        total = term_q if total is None else total + term_q
        at = pl.ds(i * ROWS, ROWS)
        split_pair(term_k + wide[:, :HD], term_v + wide[:, HD:], own_part.at[at], far_part.at[at])
    if places[-1] == 0:
        put_rows(out, total)
    else:
        out[...] = total


def finish_kernel(dq, dq_far, kept, incoming, d_query, d_key, d_value):
    d_query[...] = (dq[...] + dq_far[...].astype(F32)).astype(BF16)
    both = (kept[...] + incoming[...].astype(F32)).T
    d_key[...] = both[: HD // 2].astype(BF16)
    d_value[...] = both[HD // 2 :].astype(BF16)


def on_device(query, key_states, value_states, d_out, span_order):
    head_index = lax.axis_index("head")
    first = head_index // 2 * HD
    k_own = lax.dynamic_slice_in_dim(key_states, first, HD, 1)
    v_own = lax.dynamic_slice_in_dim(value_states, first, HD, 1)
    kv = tagged(span_order, k_own, v_own)
    qo = tagged(span_order, query, d_out)
    qo_far = far_swapped(qo)
    near = [kv, turned(kv, 1), turned(kv, 3), turned(kv, 2)]
    far = [core_swapped(block) for block in near]
    blocks = [b for pair in zip(near, far) for b in pair]
    gathered = ((8, ROWS + TAG, 2 * HD), BF16)
    stat = ((8, LANES), F32)
    here, kv = call(functools.partial(total_kernel, True), "totals", [stat, gathered], qo, *blocks)
    here_far = far_swapped(here)
    qo_far, kv, here = lax.optimization_barrier((qo_far, kv, here))
    (there,) = call(functools.partial(total_kernel, False), "totals", [stat], qo_far, kv)
    there_far = far_swapped(there)
    halves = [((ROWS, 2 * HD), F32), ((ROWS, 2 * HD), BF16)]
    wides, transposed = [((PAIR, 2 * HD), F32)] * 2, [((HD, LANES), F32)]

    def far_grads(places, *before):
        outs = (halves[1:] if places[-1] == 0 else transposed) + wides
        return call(functools.partial(far_kernel, places), "far", outs, qo_far, there, here_far, kv, *before)

    def own_grads(places, *before):
        count = len(places) * ROWS
        outs = [((count, 2 * HD), F32), ((count, 2 * HD), BF16)] + (halves[:1] if places[-1] == 0 else transposed)
        return call(functools.partial(own_kernel, places), "own", outs, qo, here, there_far, kv, *before)

    def joined(own_part, far_part):
        return (own_part + core_swapped(far_part).astype(F32)).astype(BF16)

    dq_far, *terms = far_grads((3, 2))
    *parts, dq = own_grads((3, 2), *terms)
    dq_far, *terms = far_grads((1, 0), dq_far)
    parts = joined(*parts)
    part_a, part_b = parts[:ROWS], parts[ROWS:]
    arrived = [turned(part_a, 2), turned(part_b, 1)]
    dq_there = far_swapped(dq_far)
    dq, part_a, part_b, dq_far = lax.optimization_barrier((dq, part_a, part_b, dq_far))
    *parts, dq = own_grads((1,), terms[0], dq)
    own_part, far_part, dq = own_grads((0,), terms[1], dq)
    arrived.append(turned(joined(*parts), 3))
    *arrived, dq_there = lax.optimization_barrier((*arrived, dq_there))
    grad = own_part + core_swapped(far_part).astype(F32)
    for part in arrived:
        grad = grad + part.astype(F32)
    half = HD // 2
    keep_at = head_index % 2 * half
    give_at = half - keep_at

    def cut(at):
        return jnp.concatenate([lax.dynamic_slice_in_dim(grad, first + at, half, 1) for first in (0, HD)], axis=1)

    incoming = pair_swapped(cut(give_at).astype(BF16))
    outs = [((ROWS, 2 * HD), BF16)] + [((half, ROWS), BF16)] * 2
    d_query, d_key, d_value = call(finish_kernel, "finish", outs, dq, dq_there, cut(keep_at), incoming)
    return d_query, d_key.T, d_value.T


def solution(mesh):
    return jax.shard_map(
        on_device,
        mesh=mesh,
        in_specs=(P("ctx", "head"), P("ctx", None), P("ctx", None), P("ctx", "head"), P("ctx")),
        out_specs=(P("ctx", "head"), P("ctx", "head"), P("ctx", "head")),
        check_vma=False,
    )
```

```python
import functools
import math

import jax
import jax.numpy as jnp
from jax import lax
from jax.experimental import pallas as pl
from jax.experimental.pallas import tpu as pltpu
from jax.sharding import PartitionSpec as P

HD = 128
CH = 224
ROWS = 2 * CH
PAIR = 2 * ROWS
LANES = 2 * ROWS
TAG = 16
LIMIT = 28
SCALE = HD ** (-0.5)
LOG2_SCALE = SCALE * math.log2(math.e)
HIDDEN = -3e38
LOWEST = -1e30
F32 = jnp.float32
BF16 = jnp.bfloat16
VMEM = pl.BlockSpec(memory_space=pltpu.VMEM)


def turned(block, step):
    route = [(i, i & 9 | ((i >> 1) + step & 3) << 1) for i in range(16)]
    return lax.ppermute(block, "ctx", route)


def core_swapped(block):
    return lax.ppermute(block, "ctx", [(i, i ^ 1) for i in range(16)])


def far_swapped(block):
    return lax.ppermute(block, "ctx", [(i, i ^ 8) for i in range(16)])


def pair_swapped(block):
    return lax.ppermute(block, "head", [(i, i ^ 1) for i in range(16)])


def tagged(span_order, *sides):
    width = sum(side.shape[1] for side in sides)
    tag = jnp.broadcast_to(jnp.pad(span_order.astype(BF16), (0, TAG - 2))[:, None], (TAG, width))
    return jnp.concatenate([jnp.concatenate(sides, axis=1), tag], axis=0)


def dot(a, b, dims):
    return lax.dot_general(a, b, (dims, ((), ())), preferred_element_type=F32)


def tags(ref):
    rows = ref[ROWS : ROWS + TAG, :HD].astype(F32)
    wide = [jnp.concatenate([rows[i : i + 1]] * (LANES // HD), axis=1) for i in range(2)]
    return [w.astype(jnp.int32) * CH for w in wide]


def row_positions(ref):
    low, high = tags(ref)
    lane = lax.broadcasted_iota(jnp.int32, (1, LANES), 1)
    lane = jnp.where(lane >= ROWS, lane - ROWS, lane)
    return jnp.where(lane >= CH, high + lane - CH, low + lane)


def stacked(ref, at):
    return jnp.concatenate([ref[:ROWS, at : at + HD], ref[:ROWS, at + HD : at + 2 * HD]], axis=0)


def pair_of(near, far):
    k = jnp.concatenate([near[:ROWS, :HD], far[:ROWS, :HD]], axis=0)
    v = jnp.concatenate([near[:ROWS, HD:], far[:ROWS, HD:]], axis=0)
    starts = tags(near) + tags(far)
    return k, v, starts


def total_kernel(gather, *refs):
    qo, refs = refs[0], refs[1:]
    if gather:
        blocks, stat, kv = refs[:8], refs[8], refs[9]
        for i, block in enumerate(blocks):
            kv[i] = block[...]
    else:
        kv, stat = refs
    q, o = stacked(qo, 0), stacked(qo, 2 * HD)
    at = row_positions(qo)
    key_row = lax.broadcasted_iota(jnp.int32, (CH, LANES), 0)

    def step(i, state):
        biggest, summed, weighted = state
        k, v, starts = pair_of(kv.at[2 * i], kv.at[2 * i + 1])
        score = dot(k, q, ((1,), (1,)))
        d_prob = dot(v, o, ((1,), (1,)))
        parts = []
        newest = biggest
        for j, start in enumerate(starts):
            part = score[j * CH : (j + 1) * CH] * LOG2_SCALE
            part = jnp.where(key_row <= at - start, part, HIDDEN).reshape(CH // 8, 8, LANES)
            newest = jnp.maximum(newest, jnp.max(part, axis=0))
            parts.append(part)
        factor = jnp.exp2(biggest - newest)
        summed = summed * factor
        weighted = weighted * factor
        for j, part in enumerate(parts):
            expo = jnp.exp2(part - newest[None])
            summed += jnp.sum(expo, axis=0)
            weighted += jnp.sum(expo * d_prob[j * CH : (j + 1) * CH].reshape(CH // 8, 8, LANES), axis=0)
        return newest, summed, weighted

    nothing = jnp.zeros((8, LANES), F32)
    biggest, summed, weighted = lax.fori_loop(0, 4, step, (nothing + LOWEST, nothing, nothing))
    top = jnp.max(biggest, axis=0, keepdims=True)
    factor = jnp.exp2(biggest - top)
    stat[0:1] = top
    stat[1:2] = jnp.sum(summed * factor, axis=0, keepdims=True)
    stat[2:3] = jnp.sum(weighted * factor, axis=0, keepdims=True)
    stat[3:8] = jnp.zeros((5, LANES), F32)


def call(kernel, name, outs, *operands):
    return pl.pallas_call(
        kernel,
        out_shape=[jax.ShapeDtypeStruct(*out) for out in outs],
        in_specs=[VMEM] * len(operands),
        out_specs=[VMEM] * len(outs),
        compiler_params=pltpu.CompilerParams(vmem_limit_bytes=LIMIT << 20),
        cost_estimate=pl.CostEstimate(flops=1 << 20, bytes_accessed=1 << 16, transcendentals=0),
        name=name,
    )(*operands)


def merged(here, there):
    top = jnp.maximum(here[0:1], there[0:1])
    mine, other = jnp.exp2(here[0:1] - top), jnp.exp2(there[0:1] - top)
    summed = here[1:2] * mine + there[1:2] * other
    weighted = here[2:3] * mine + there[2:3] * other
    return top + jnp.log2(summed), weighted / summed


def rows_of(qo, here, there):
    return stacked(qo, 0), stacked(qo, 2 * HD), row_positions(qo), *merged(here, there)


def tile(rows, near, far):
    q, o, at, lse, delta = rows
    k, v, starts = pair_of(near, far)
    key_row = lax.broadcasted_iota(jnp.int32, (CH, LANES), 0)
    score = dot(k, q, ((1,), (1,)))
    d_prob = dot(v, o, ((1,), (1,)))
    probs, d_scores = [], []
    for j, start in enumerate(starts):
        here = slice(j * CH, (j + 1) * CH)
        prob = jnp.exp2(score[here] * LOG2_SCALE - lse)
        prob = jnp.where(key_row <= at - start, prob, 0.0)
        d_scores.append((prob * (d_prob[here] - delta)).astype(BF16))
        probs.append(prob.astype(BF16))
    d_score = jnp.concatenate(d_scores, axis=0)
    prob = jnp.concatenate(probs, axis=0)
    return (
        dot(d_score, q, ((1,), (0,))) * SCALE,
        dot(prob, o, ((1,), (0,))),
        dot(k, d_score, ((0,), (0,))) * SCALE,
    )


def split_pair(term_k, term_v, own_part, far_part):
    own_part[:, :HD] = term_k[:ROWS]
    own_part[:, HD:] = term_v[:ROWS]
    far_part[:, :HD] = term_k[ROWS:].astype(BF16)
    far_part[:, HD:] = term_v[ROWS:].astype(BF16)


def put_rows(out, dq):
    rows = dq.T
    out[:, :HD] = rows[:ROWS].astype(out.dtype)
    out[:, HD:] = rows[ROWS:].astype(out.dtype)


def far_kernel(places, qo_far, here, there, kv, *refs):
    out, *terms = refs
    rows = rows_of(qo_far, here, there)
    total = None
    for place, wide in zip(places, terms):
        term_k, term_v, term_q = tile(rows, kv.at[2 * place], kv.at[2 * place + 1])
        wide[:, :HD] = term_k
        wide[:, HD:] = term_v
        total = term_q if total is None else total + term_q
    if places[-1] == 0:
        put_rows(out, total)
    else:
        out[...] = total


def own_kernel(places, qo, here, there, kv, *refs):
    terms, refs = refs[: len(places)], refs[len(places) :]
    own_part, far_part, out = refs[-3:]
    rows = rows_of(qo, here, there)
    total = refs[0][...] if len(refs) > 3 else None
    for i, (place, wide) in enumerate(zip(places, terms)):
        term_k, term_v, term_q = tile(rows, kv.at[2 * place], kv.at[2 * place + 1])
        total = term_q if total is None else total + term_q
        at = pl.ds(i * ROWS, ROWS)
        split_pair(term_k + wide[:, :HD], term_v + wide[:, HD:], own_part.at[at], far_part.at[at])
    if places[-1] == 0:
        put_rows(out, total)
    else:
        out[...] = total


def finish_kernel(dq, dq_far, kept, incoming, d_query, d_key, d_value):
    d_query[...] = (dq[...] + dq_far[...].astype(F32)).astype(BF16)
    both = (kept[...] + incoming[...].astype(F32)).T
    d_key[...] = both[: HD // 2].astype(BF16)
    d_value[...] = both[HD // 2 :].astype(BF16)


def on_device(query, key_states, value_states, d_out, span_order):
    head_index = lax.axis_index("head")
    first = head_index // 2 * HD
    k_own = lax.dynamic_slice_in_dim(key_states, first, HD, 1)
    v_own = lax.dynamic_slice_in_dim(value_states, first, HD, 1)
    kv = tagged(span_order, k_own, v_own)
    qo = tagged(span_order, query, d_out)
    qo_far = far_swapped(qo)
    near = [kv, turned(kv, 1), turned(kv, 3), turned(kv, 2)]
    far = [core_swapped(block) for block in near]
    blocks = [b for pair in zip(near, far) for b in pair]
    gathered = ((8, ROWS + TAG, 2 * HD), BF16)
    stat = ((8, LANES), F32)
    here, kv = call(functools.partial(total_kernel, True), "totals", [stat, gathered], qo, *blocks)
    here_far = far_swapped(here)
    qo_far, kv, here = lax.optimization_barrier((qo_far, kv, here))
    (there,) = call(functools.partial(total_kernel, False), "totals", [stat], qo_far, kv)
    there_far = far_swapped(there)
    halves = [((ROWS, 2 * HD), F32), ((ROWS, 2 * HD), BF16)]
    wides, transposed = [((PAIR, 2 * HD), F32)] * 2, [((HD, LANES), F32)]

    def far_grads(places, *before):
        outs = (halves[1:] if places[-1] == 0 else transposed) + wides * 2
        return call(functools.partial(far_kernel, places), "far", outs, qo_far, there, here_far, kv, *before)

    def own_grads(places, *before):
        count = len(places) * ROWS
        outs = [((count, 2 * HD), F32), ((count, 2 * HD), BF16)] + (halves[:1] if places[-1] == 0 else transposed)
        return call(functools.partial(own_kernel, places), "own", outs, qo, here, there_far, kv, *before)

    def joined(own_part, far_part):
        return (own_part + core_swapped(far_part).astype(F32)).astype(BF16)

    dq_far, *terms = far_grads((3, 2, 1, 0))
    dq_there = far_swapped(dq_far)
    terms[0], dq_far = lax.optimization_barrier((terms[0], dq_far))
    *parts, dq = own_grads((3, 2), *terms[:2])
    *part_c, dq = own_grads((1,), terms[2], dq)
    parts = joined(*parts)
    part_a, part_b = parts[:ROWS], parts[ROWS:]
    arrived = [turned(part_a, 2), turned(part_b, 1)]
    dq, part_a, part_b = lax.optimization_barrier((dq, part_a, part_b))
    own_part, far_part, dq = own_grads((0,), terms[3], dq)
    arrived.append(turned(joined(*part_c), 3))
    *arrived, dq_there = lax.optimization_barrier((*arrived, dq_there))
    grad = own_part + core_swapped(far_part).astype(F32)
    for part in arrived:
        grad = grad + part.astype(F32)
    half = HD // 2
    keep_at = head_index % 2 * half
    give_at = half - keep_at

    def cut(at):
        return jnp.concatenate([lax.dynamic_slice_in_dim(grad, first + at, half, 1) for first in (0, HD)], axis=1)

    incoming = pair_swapped(cut(give_at).astype(BF16))
    outs = [((ROWS, 2 * HD), BF16)] + [((half, ROWS), BF16)] * 2
    d_query, d_key, d_value = call(finish_kernel, "finish", outs, dq, dq_there, cut(keep_at), incoming)
    return d_query, d_key.T, d_value.T


def solution(mesh):
    return jax.shard_map(
        on_device,
        mesh=mesh,
        in_specs=(P("ctx", "head"), P("ctx", None), P("ctx", None), P("ctx", "head"), P("ctx")),
        out_specs=(P("ctx", "head"), P("ctx", "head"), P("ctx", "head")),
        check_vma=False,
    )
```
